32 devices in a mesh: row: 8 (over y, x, core), col: 4 (over z).
Axes of the slice: x: 2, y: 2, z: 4, core: 2. Of those that a mesh axis runs over, the one named last changes fastest.
Arguments:
- features: bfloat16 [4096, 512], P(('row', 'col')), may hold values from -6 to 6
- coefs: bfloat16 [4096], P(('row', 'col')), may hold values from -150 to 150
Outputs:
- grads: bfloat16 [4096, 512], P(('row', 'col'))
- recolored: bfloat16 [4096, 512], P(('row', 'col'))
The draws below stay inside these ranges and needn't reach their ends.
All inputs are finite; a program needn't handle non-finite values.
Results may differ from the reference program's by a relative error of at most 0.0025.
The reference program's roundings to bfloat16 on the way (of `kernel`, `weighted` and `agop`) count: a program that leaves them out, or rounds other values in their place, can miss the bound.
Values may be sent and summed in bfloat16 or wider, within the bound.
A program may use at most 64 MiB of HBM per device.

```python
import jax
import jax.numpy as jnp
from jax import lax

D = 512
NPTS = 4096


def block_scale(rng, extent, pieces, smallest, largest):
    factor_of, own = 1.0, jax.random.fold_in(rng, 6)
    for axis_at, shards_of in pieces:
        steps = jnp.exp(jax.random.uniform(jax.random.fold_in(own, axis_at), (shards_of,), jnp.float32, smallest / len(pieces), largest / len(pieces)))
        factor_of = factor_of * jnp.repeat(steps, extent[axis_at] // shards_of).reshape([-1 if axis == axis_at else 1 for axis in range(len(extent))])
    return factor_of


def scatter_about(rng, extent, scale, most, shards=(), kind=jnp.bfloat16):
    gain = block_scale(rng, extent, shards, -0.22, 0.18) if shards else 1.0
    result = jax.random.normal(rng, extent, jnp.float32) * scale * gain
    return jnp.minimum(jnp.maximum(result, -most), most).astype(kind)


def setup_inputs(seed: int = 0) -> dict:
    arg_keys = jax.random.split(jax.random.key(seed), 3)
    return {
        "features": scatter_about(arg_keys[0], (NPTS, D), 1.0, 6.0, ((0, 32),)),
        "coefs": scatter_about(arg_keys[1], (NPTS,), 25.0, 150.0, ((0, 32),)),
    }


def reference(features, coefs):
    width = features.shape[1]
    gamma = 2.0 / width
    feats_full = features.astype(jnp.float32)
    coef_full = coefs.astype(jnp.float32)
    norms = jnp.sum(feats_full * feats_full, axis=1)
    weighted = (coef_full[:, None] * feats_full).astype(jnp.bfloat16)
    weighted_full = lax.optimization_barrier(weighted).astype(jnp.float32)
    strip_len = min(512, NPTS)
    strip_count = NPTS // strip_len

    def one_strip(packed):
        strip_feats, strip_norms = packed
        products = jnp.dot(strip_feats, feats_full.T, precision=lax.Precision.HIGHEST)
        kernel = jnp.exp(-(strip_norms[:, None] + norms[None, :] - 2.0 * products) * gamma).astype(jnp.bfloat16)
        kernel_full = lax.optimization_barrier(kernel).astype(jnp.float32)
        totals = jnp.dot(kernel_full, coef_full, precision=lax.Precision.HIGHEST)
        moments = jnp.dot(kernel_full, weighted_full, precision=lax.Precision.HIGHEST)
        return totals, moments

    totals, moments = lax.map(one_strip, (feats_full.reshape(strip_count, strip_len, width), norms.reshape(strip_count, strip_len)))
    totals = totals.reshape(NPTS)
    moments = moments.reshape(NPTS, width)
    grads = (2.0 * gamma * (moments - totals[:, None] * feats_full)).astype(jnp.bfloat16)
    grads_full = lax.optimization_barrier(grads).astype(jnp.float32)
    gram = jnp.dot(grads_full.T, grads_full, precision=lax.Precision.HIGHEST)
    agop = (gram / NPTS).astype(jnp.bfloat16)
    agop_full = lax.optimization_barrier(agop).astype(jnp.float32)
    recolored = jnp.dot(feats_full, agop_full, precision=lax.Precision.HIGHEST).astype(jnp.bfloat16)
    return grads, recolored
```

```python
import functools

import jax
import jax.numpy as jnp
from jax import lax
from jax.experimental import pallas as pl
from jax.experimental.pallas import tpu as pltpu
from jax.sharding import PartitionSpec as P

MESH = pl.DeviceIdType.MESH
NT = (((1,), (1,)), ((), ()))
TN = (((0,), (0,)), ((), ()))


def flipped(value, bits):
    bit = 1
    while bit <= bits:
        if bits & bit:
            value = value + bit - 2 * bit * lax.rem(lax.div(value, bit), 2)
        bit *= 2
    return value


def kernel(
    planes, cols, point_count,
    feat_ref, coef_ref, grads_ref, rec_ref,
    rows, buf, info, norms, mom, tot, part, part_in, whole_grads,
    gram, gram_out, gram_in, agop, rec_out, rec_in,
    sib_s, sib_r, info_s, info_r, blk_s, blk_r, diag_s, diag_r,
    part_s, part_r, gram_s, gram_r, agop_s, agop_r, rec_s, rec_r,
):
    count, width = feat_ref.shape
    gamma = 2.0 / width
    half = width // 2
    chips = planes * cols
    row = lax.axis_index("row")
    z = lax.axis_index("col")
    p, core = lax.div(row, 2), lax.rem(row, 2)
    peers = [(d, k) for k in range(cols) for d in range(planes) if (d, k) != (0, 0)]

    def chip(d, k):
        return (flipped(p, d) * 2 + core, flipped(z, k))

    sibling = (flipped(row, 1), z)

    def copy(src, dst, send, recv, device):
        return pltpu.make_async_remote_copy(
            src_ref=src, dst_ref=dst, send_sem=send, recv_sem=recv,
            device_id=device, device_id_type=MESH,
        )

    barrier = pltpu.get_barrier_semaphore()
    pl.semaphore_signal(barrier, inc=1, device_id=sibling, device_id_type=MESH)
    for d, k in peers:
        pl.semaphore_signal(barrier, inc=1, device_id=chip(d, k), device_id_type=MESH)

    own_full = feat_ref[...].astype(jnp.float32)
    own_norms = jnp.sum(own_full * own_full, axis=1, keepdims=True)
    info[0, 0, 0:1, :] = coef_ref[...]
    info[0, 0, 1:2, :] = jnp.transpose(jnp.broadcast_to(own_norms, (count, 128)))[0:1, :]
    info[0, 0, 2:8, :] = jnp.zeros((6, count), jnp.float32)
    rows[pl.ds(core, 1)] = feat_ref[...][None]
    mom[...] = jnp.zeros_like(mom)
    tot[...] = jnp.zeros_like(tot)
    pl.semaphore_wait(barrier, chips)

    sent = []

    def send(*args):
        made = copy(*args)
        made.start()
        sent.append(made)
        return made

    from_sib = send(feat_ref, rows.at[core], sib_s, sib_r, sibling)
    blocks, diagonals, infos = {}, {}, {}
    relay = planes == 4

    def spread(k):
        for e in ((1, 2) if relay else range(1, planes)):
            source = feat_ref if k == 0 else buf.at[0, k]
            blocks[e, k] = send(source, buf.at[e, k], blk_s.at[e, k], blk_r.at[e, k], chip(e, 0))

    def forward(k):
        upper, lower = pl.ds(0, count // 2), pl.ds(count // 2, count // 2)
        blocks[1, k].wait_recv()
        blocks[3, k] = send(
            buf.at[1, k, upper], buf.at[3, k, upper], blk_s.at[3, k], blk_r.at[3, k], chip(2, 0)
        )
        blocks[2, k].wait_recv()
        diagonals[k] = send(
            buf.at[2, k, lower], buf.at[3, k, lower], diag_s.at[k], diag_r.at[k], chip(1, 0)
        )

    for k in range(1, cols):
        blocks[0, k] = send(feat_ref, buf.at[0, k], blk_s.at[0, k], blk_r.at[0, k], chip(0, k))
    spread(0)
    for d, k in peers:
        infos[d, k] = send(
            info.at[0, 0], info.at[d, k], info_s.at[d, k], info_r.at[d, k], chip(d, k)
        )

    from_sib.wait_recv()
    both = rows[...].reshape(2 * count, width)
    both_full = both.astype(jnp.float32)
    norms[...] = jnp.sum(both_full * both_full, axis=1, keepdims=True)

    def add_block(points, facts):
        coefs = facts[0:1, :]
        col_norms = facts[1:2, :]
        products = lax.dot_general(
            rows[...].reshape(2 * count, width), points, NT, preferred_element_type=jnp.float32
        )
        kern = jnp.exp(-(norms[...] + col_norms - 2.0 * products) * gamma).astype(jnp.bfloat16)
        tall = jnp.transpose(jnp.broadcast_to(coefs, (128, count)))[:, 0:1]
        weighted = (tall * points.astype(jnp.float32)).astype(jnp.bfloat16)
        tot[...] += kern.astype(jnp.float32) * coefs
        mom[...] += jnp.dot(kern, weighted, preferred_element_type=jnp.float32)

    add_block(feat_ref[...], info[0, 0])
    if relay:
        def take(d, k):
            infos[d, k].wait_recv()
            if d == 3:
                blocks[d, k].wait_recv()
                diagonals[k].wait_recv()
            add_block(buf[d, k], info[d, k])

        for k in range(1, cols + 1):
            if k < cols:
                blocks[0, k].wait_recv()
                spread(k)
            forward(k - 1)
            if k < cols:
                take(0, k)
            take(1, k - 1)
            take(2, k - 1)
            if k > 1:
                take(3, k - 2)
        take(3, cols - 1)
    else:
        for k in range(1, cols):
            blocks[0, k].wait_recv()
            spread(k)
        for d, k in peers:
            infos[d, k].wait_recv()
            if d:
                blocks[d, k].wait_recv()

        @pl.loop(1, chips)
        def _(at):
            d, k = lax.div(at, cols), lax.rem(at, cols)
            add_block(buf[d, k], info[d, k])

    totals = jnp.sum(tot[...], axis=1, keepdims=True)
    part[...] = mom[...] - totals * rows[...].reshape(2 * count, width).astype(jnp.float32)
    send(part, part_in, part_s, part_r, sibling).wait_recv()
    both_grads = (2.0 * gamma * (part[...] + part_in[...])).astype(jnp.bfloat16)
    whole_grads[...] = both_grads
    grads_ref[...] = whole_grads[pl.ds(pl.multiple_of(core * count, count), count), :]

    owners, depth = gram.shape[0], gram.shape[1]
    mine = pl.ds(pl.multiple_of(core * half, half), half)
    product = lax.dot_general(
        whole_grads[:, mine], whole_grads[...], TN, preferred_element_type=jnp.float32
    )
    gram[...] = product.reshape(owners, depth, width)
    gram_out[...] = product.astype(jnp.bfloat16).reshape(owners, depth, width)

    me = p * cols + z
    every = owners == chips

    def owning(index, do):
        if every:
            do()
        else:
            pl.when(index < owners)(do)

    def place(index):
        return index if every else lax.rem(index, owners)

    def gram_copy(d, k):
        return copy(
            gram_out.at[place(flipped(p, d) * cols + flipped(z, k))], gram_in.at[d, k],
            gram_s.at[d, k], gram_r.at[d, k], chip(d, k),
        )

    def agop_copy(d, k):
        at = agop.at[place(me)]
        return copy(at, at, agop_s.at[d, k], agop_r.at[d, k], chip(d, k))

    for d, k in peers:
        owning(flipped(p, d) * cols + flipped(z, k), gram_copy(d, k).start)

    def reduce_own():
        total = gram[place(me)]
        for d, k in peers:
            gram_copy(d, k).wait_recv()
            total += gram_in[d, k].astype(jnp.float32)
        agop[place(me)] = (total / point_count).astype(jnp.bfloat16)
        for d, k in peers:
            agop_copy(d, k).start()

    owning(me, reduce_own)
    for d, k in peers:
        owning(flipped(p, d) * cols + flipped(z, k), agop_copy(d, k).wait_recv)

    colored = lax.dot_general(
        rows[...].reshape(2 * count, width), agop[...].reshape(half, width), NT,
        preferred_element_type=jnp.float32,
    ).astype(jnp.bfloat16).reshape(2, count, half)
    rec_out[...] = colored
    swap = send(rec_out.at[1 - core], rec_in, rec_s, rec_r, sibling)
    rec_ref[:, mine] = rec_out[core]
    swap.wait_recv()
    rec_ref[:, pl.ds(pl.multiple_of((1 - core) * half, half), half)] = rec_in[...]

    for made in sent:
        made.wait_send()
    for d, k in peers:
        owning(flipped(p, d) * cols + flipped(z, k), gram_copy(d, k).wait_send)

    def agop_sent():
        for d, k in peers:
            agop_copy(d, k).wait_send()

    owning(me, agop_sent)


def local(planes, cols, features, coefs):
    count, width = features.shape
    chips = planes * cols
    half = width // 2
    owners = min(chips, half // 16)
    depth = half // owners
    bf16, f32 = jnp.bfloat16, jnp.float32
    dma = pltpu.SemaphoreType.DMA
    vmem = pltpu.VMEM
    return pl.pallas_call(
        functools.partial(kernel, planes, cols, count * chips * 2),
        out_shape=[jax.ShapeDtypeStruct((count, width), bf16)] * 2,
        in_specs=[pl.BlockSpec(memory_space=vmem)] * 2,
        out_specs=[pl.BlockSpec(memory_space=vmem)] * 2,
        scratch_shapes=[
            vmem((2, count, width), bf16),
            vmem((planes, cols, count, width), bf16),
            vmem((planes, cols, 8, count), f32),
            vmem((2 * count, 1), f32),
            vmem((2 * count, width), f32),
            vmem((2 * count, count), f32),
            vmem((2 * count, width), f32),
            vmem((2 * count, width), f32),
            vmem((2 * count, width), bf16),
            vmem((owners, depth, width), f32),
            vmem((owners, depth, width), bf16),
            vmem((planes, cols, depth, width), bf16),
            vmem((owners, depth, width), bf16),
            vmem((2, count, half), bf16),
            vmem((count, half), bf16),
            dma(()), dma(()),
            dma((planes, cols)), dma((planes, cols)),
            dma((planes, cols)), dma((planes, cols)),
            dma((cols,)), dma((cols,)),
            dma(()), dma(()),
            dma((planes, cols)), dma((planes, cols)),
            dma((planes, cols)), dma((planes, cols)),
            dma(()), dma(()),
        ],
        compiler_params=pltpu.CompilerParams(
            collective_id=0, has_side_effects=True, vmem_limit_bytes=40 * 1024 * 1024
        ),
        cost_estimate=pl.CostEstimate(
            flops=8 * count * count * chips * width,
            bytes_accessed=6 * count * width,
            transcendentals=2 * count * count * chips,
        ),
    )(features, coefs.astype(f32).reshape(1, count))


def solution(mesh):
    return jax.shard_map(
        functools.partial(local, mesh.shape["row"] // 2, mesh.shape["col"]),
        mesh=mesh,
        in_specs=(P(("row", "col"), None), P(("row", "col"))),
        out_specs=(P(("row", "col"), None), P(("row", "col"), None)),
        check_vma=False,
    )
```

```python
import functools

import jax
import jax.numpy as jnp
from jax import lax
from jax.experimental import pallas as pl
from jax.experimental.pallas import tpu as pltpu
from jax.sharding import PartitionSpec as P

MESH = pl.DeviceIdType.MESH
NT = (((1,), (1,)), ((), ()))
TN = (((0,), (0,)), ((), ()))


def flipped(value, bits):
    bit = 1
    while bit <= bits:
        if bits & bit:
            value = value + bit - 2 * bit * lax.rem(lax.div(value, bit), 2)
        bit *= 2
    return value


def slot_of(z, block, cols):
    far = jnp.abs(block - z)
    both = jnp.minimum(z, cols - 1 - z)
    left = (block < z).astype(jnp.int32)
    return jnp.where(far <= both, 2 * far - left, far + both)


def arrival(z, slot, cols):
    both = jnp.minimum(z, cols - 1 - z)
    paired = slot <= 2 * both
    far = jnp.where(paired, (slot + 1) // 2, slot - both)
    left = jnp.where(paired, slot % 2, (2 * z >= cols).astype(jnp.int32))
    return z + far - 2 * far * left, left


def kernel(
    planes, cols, point_count,
    feat_hbm, coef_hbm, grads_ref, rec_ref,
    feat_ref, coef_ref, in_s,
    rows, buf, info, norms, mom, tot, part, part_in, whole_grads,
    gram, gram_out, gram_in, agop, rec_out, rec_in,
    line_s, sib_s, sib_r, info_s, info_r, blk_s, blk_r, diag_s, diag_r,
    part_s, part_r, gram_s, gram_r, agop_s, agop_r, rec_s, rec_r,
):
    load_feats = pltpu.make_async_copy(feat_hbm, feat_ref, in_s.at[0])
    load_coefs = pltpu.make_async_copy(coef_hbm, coef_ref, in_s.at[1])
    load_feats.start()
    load_coefs.start()
    count, width = feat_ref.shape
    gamma = 2.0 / width
    half = width // 2
    chips = planes * cols
    row = lax.axis_index("row")
    z = lax.axis_index("col")
    p, core = lax.div(row, 2), lax.rem(row, 2)
    peers = [(d, k) for k in range(cols) for d in range(planes) if (d, k) != (0, 0)]

    def chip(d, k):
        return (flipped(p, d) * 2 + core, flipped(z, k))

    sibling = (flipped(row, 1), z)

    def copy(src, dst, send, recv, device):
        return pltpu.make_async_remote_copy(
            src_ref=src, dst_ref=dst, send_sem=send, recv_sem=recv,
            device_id=device, device_id_type=MESH,
        )

    barrier = pltpu.get_barrier_semaphore()
    relay = planes == 4
    beside = (1, 2) if relay else range(1, planes)

    def greet(device):
        pl.semaphore_signal(barrier, inc=1, device_id=device, device_id_type=MESH)

    greet(sibling)
    for e in beside:
        greet(chip(e, 0))
    pl.when(z > 0)(lambda: greet((row, z - 1)))
    pl.when(z < cols - 1)(lambda: greet((row, z + 1)))

    load_feats.wait()
    load_coefs.wait()
    own_full = feat_ref[...].astype(jnp.float32)
    own_norms = jnp.sum(own_full * own_full, axis=1, keepdims=True)
    info[0, 0, 0:1, :] = coef_ref[...].astype(jnp.float32)
    info[0, 0, 1:2, :] = jnp.transpose(jnp.broadcast_to(own_norms, (count, 128)))[0:1, :]
    rows[pl.ds(core, 1)] = feat_ref[...][None]
    mom[...] = jnp.zeros_like(mom)
    tot[...] = jnp.zeros_like(tot)
    on_line = (z > 0).astype(jnp.int32) + (z < cols - 1).astype(jnp.int32)
    pl.semaphore_wait(barrier, 1 + len(beside) + on_line)

    sent = []

    def send(*args):
        made = copy(*args)
        made.start()
        sent.append(made)
        return made

    from_sib = send(feat_ref, rows.at[core], sib_s, sib_r, sibling)
    blocks, diagonals, infos = {}, {}, {}

    def spread(k):
        for e in beside:
            infos[e, k] = send(
                info.at[0, k], info.at[e, k], info_s.at[e, k], info_r.at[e, k], chip(e, 0)
            )
            source = feat_ref if k == 0 else buf.at[0, k]
            blocks[e, k] = send(source, buf.at[e, k], blk_s.at[e, k], blk_r.at[e, k], chip(e, 0))

    def forward(k):
        upper, lower = pl.ds(0, count // 2), pl.ds(count // 2, count // 2)
        infos[1, k].wait_recv()
        infos[3, k] = send(
            info.at[1, k], info.at[3, k], info_s.at[3, k], info_r.at[3, k], chip(2, 0)
        )
        blocks[1, k].wait_recv()
        blocks[3, k] = send(
            buf.at[1, k, upper], buf.at[3, k, upper], blk_s.at[3, k], blk_r.at[3, k], chip(2, 0)
        )
        blocks[2, k].wait_recv()
        diagonals[k] = send(
            buf.at[2, k, lower], buf.at[3, k, lower], diag_s.at[k], diag_r.at[k], chip(1, 0)
        )

    def along(k, block, to, sem):
        slot = slot_of(to, block, cols)
        facts = copy(info.at[0, k], info.at[0, slot], sem(1), info_r.at[0, slot], (row, to))
        source = feat_ref if k == 0 else buf.at[0, k]
        return facts, copy(source, buf.at[0, slot], sem(0), blk_r.at[0, slot], (row, to))

    def line(do):
        def to_right():
            for made in along(0, z, z + 1, lambda at: line_s.at[0, at]):
                do(made)

        def to_left():
            for made in along(0, z, z - 1, lambda at: line_s.at[1, at]):
                do(made)

        pl.when(z < cols - 1)(to_right)
        pl.when(z > 0)(to_left)

    def onward(k, do):
        block, left = arrival(z, k, cols)
        to = z - 1 + 2 * left

        def both():
            for made in along(k, block, to, lambda at: (info_s if at else blk_s).at[0, k]):
                do(made)

        pl.when(jnp.logical_and(to >= 0, to < cols))(both)

    def arrived(k):
        copy(info.at[0, 0], info.at[0, k], info_s.at[0, k], info_r.at[0, k], sibling).wait_recv()
        copy(feat_ref, buf.at[0, k], blk_s.at[0, k], blk_r.at[0, k], sibling).wait_recv()

    line(lambda made: made.start())
    spread(0)

    from_sib.wait_recv()
    both = rows[...].reshape(2 * count, width)
    both_full = both.astype(jnp.float32)
    norms[...] = jnp.sum(both_full * both_full, axis=1, keepdims=True)

    def add_block(points, facts):
        coefs = facts[0:1, :]
        col_norms = facts[1:2, :]
        products = lax.dot_general(
            rows[...].reshape(2 * count, width), points, NT, preferred_element_type=jnp.float32
        )
        kern = jnp.exp(-(norms[...] + col_norms - 2.0 * products) * gamma).astype(jnp.bfloat16)
        tall = jnp.transpose(jnp.broadcast_to(coefs, (128, count)))[:, 0:1]
        weighted = (tall * points.astype(jnp.float32)).astype(jnp.bfloat16)
        tot[...] += kern.astype(jnp.float32) * coefs
        mom[...] += jnp.dot(kern, weighted, preferred_element_type=jnp.float32)

    add_block(feat_ref[...], info[0, 0])
    if relay:
        def take(d, k):
            if d > 1:
                infos[d, k].wait_recv()
            if d == 3:
                blocks[d, k].wait_recv()
                diagonals[k].wait_recv()
            add_block(buf[d, k], info[d, k])

        for k in range(1, cols + 1):
            if k < cols:
                arrived(k)
                onward(k, lambda made: made.start())
                spread(k)
            forward(k - 1)
            if k < cols:
                take(0, k)
            take(1, k - 1)
            take(2, k - 1)
            if k > 1:
                take(3, k - 2)
        take(3, cols - 1)
    else:
        for k in range(1, cols):
            arrived(k)
            onward(k, lambda made: made.start())
            spread(k)
        for d, k in peers:
            if d:
                infos[d, k].wait_recv()
                blocks[d, k].wait_recv()

        @pl.loop(1, chips)
        def _(at):
            d, k = lax.div(at, cols), lax.rem(at, cols)
            add_block(buf[d, k], info[d, k])

    totals = jnp.sum(tot[...], axis=1, keepdims=True)
    part[...] = mom[...] - totals * rows[...].reshape(2 * count, width).astype(jnp.float32)
    send(part, part_in, part_s, part_r, sibling).wait_recv()
    both_grads = (2.0 * gamma * (part[...] + part_in[...])).astype(jnp.bfloat16)
    whole_grads[...] = both_grads
    grads_ref[...] = whole_grads[pl.ds(pl.multiple_of(core * count, count), count), :]

    owners, depth = gram.shape[0], gram.shape[1]
    mine = pl.ds(pl.multiple_of(core * half, half), half)
    product = lax.dot_general(
        whole_grads[:, mine], whole_grads[...], TN, preferred_element_type=jnp.float32
    )
    gram[...] = product.reshape(owners, depth, width)
    gram_out[...] = product.astype(jnp.bfloat16).reshape(owners, depth, width)

    me = p * cols + z
    every = owners == chips

    def owning(index, do):
        if every:
            do()
        else:
            pl.when(index < owners)(do)

    def place(index):
        return index if every else lax.rem(index, owners)

    def gram_copy(d, k):
        return copy(
            gram_out.at[place(flipped(p, d) * cols + flipped(z, k))], gram_in.at[d, k],
            gram_s.at[d, k], gram_r.at[d, k], chip(d, k),
        )

    def agop_copy(d, k):
        at = agop.at[place(me)]
        return copy(at, at, agop_s.at[d, k], agop_r.at[d, k], chip(d, k))

    for d, k in peers:
        owning(flipped(p, d) * cols + flipped(z, k), gram_copy(d, k).start)

    def reduce_own():
        total = gram[place(me)]
        for d, k in peers:
            gram_copy(d, k).wait_recv()
            total += gram_in[d, k].astype(jnp.float32)
        agop[place(me)] = (total / point_count).astype(jnp.bfloat16)
        for d, k in peers:
            agop_copy(d, k).start()

    owning(me, reduce_own)
    for d, k in peers:
        owning(flipped(p, d) * cols + flipped(z, k), agop_copy(d, k).wait_recv)

    colored = lax.dot_general(
        rows[...].reshape(2 * count, width), agop[...].reshape(half, width), NT,
        preferred_element_type=jnp.float32,
    ).astype(jnp.bfloat16).reshape(2, count, half)
    rec_out[...] = colored
    swap = send(rec_out.at[1 - core], rec_in, rec_s, rec_r, sibling)
    rec_ref[:, mine] = rec_out[core]
    swap.wait_recv()
    rec_ref[:, pl.ds(pl.multiple_of((1 - core) * half, half), half)] = rec_in[...]

    for made in sent:
        made.wait_send()
    line(lambda made: made.wait_send())
    for k in range(1, cols):
        onward(k, lambda made: made.wait_send())
    for d, k in peers:
        owning(flipped(p, d) * cols + flipped(z, k), gram_copy(d, k).wait_send)

    def agop_sent():
        for d, k in peers:
            agop_copy(d, k).wait_send()

    owning(me, agop_sent)


def local(planes, cols, features, coefs):
    count, width = features.shape
    chips = planes * cols
    half = width // 2
    owners = min(chips, half // 16)
    depth = half // owners
    bf16, f32 = jnp.bfloat16, jnp.float32
    dma = pltpu.SemaphoreType.DMA
    vmem = pltpu.VMEM
    return pl.pallas_call(
        functools.partial(kernel, planes, cols, count * chips * 2),
        out_shape=[jax.ShapeDtypeStruct((count, width), bf16)] * 2,
        in_specs=[pl.BlockSpec(memory_space=pl.ANY)] * 2,
        out_specs=[pl.BlockSpec(memory_space=vmem)] * 2,
        scratch_shapes=[
            vmem((count, width), bf16),
            vmem((1, count), bf16),
            dma((2,)),
            vmem((2, count, width), bf16),
            vmem((planes, cols, count, width), bf16),
            vmem((planes, cols, 2, count), f32),
            vmem((2 * count, 1), f32),
            vmem((2 * count, width), f32),
            vmem((2 * count, count), f32),
            vmem((2 * count, width), f32),
            vmem((2 * count, width), f32),
            vmem((2 * count, width), bf16),
            vmem((owners, depth, width), f32),
            vmem((owners, depth, width), bf16),
            vmem((planes, cols, depth, width), bf16),
            vmem((owners, depth, width), bf16),
            vmem((2, count, half), bf16),
            vmem((count, half), bf16),
            dma((2, 2)),
            dma(()), dma(()),
            dma((planes, cols)), dma((planes, cols)),
            dma((planes, cols)), dma((planes, cols)),
            dma((cols,)), dma((cols,)),
            dma(()), dma(()),
            dma((planes, cols)), dma((planes, cols)),
            dma((planes, cols)), dma((planes, cols)),
            dma(()), dma(()),
        ],
        compiler_params=pltpu.CompilerParams(
            collective_id=0, has_side_effects=True, vmem_limit_bytes=40 * 1024 * 1024
        ),
        cost_estimate=pl.CostEstimate(
            flops=8 * count * count * chips * width,
            bytes_accessed=6 * count * width,
            transcendentals=2 * count * count * chips,
        ),
    )(features, coefs.reshape(1, count))


def solution(mesh):
    return jax.shard_map(
        functools.partial(local, mesh.shape["row"] // 2, mesh.shape["col"]),
        mesh=mesh,
        in_specs=(P(("row", "col"), None), P(("row", "col"))),
        out_specs=(P(("row", "col"), None), P(("row", "col"), None)),
        check_vma=False,
    )
```

```python
import functools

import jax
import jax.numpy as jnp
from jax import lax
from jax.experimental import pallas as pl
from jax.experimental.pallas import tpu as pltpu
from jax.sharding import PartitionSpec as P

MESH = pl.DeviceIdType.MESH
NT = (((1,), (1,)), ((), ()))
TN = (((0,), (0,)), ((), ()))


def flipped(value, bits):
    bit = 1
    while bit <= bits:
        if bits & bit:
            value = value + bit - 2 * bit * lax.rem(lax.div(value, bit), 2)
        bit *= 2
    return value


def slot_of(z, block, cols):
    far = jnp.abs(block - z)
    both = jnp.minimum(z, cols - 1 - z)
    left = (block < z).astype(jnp.int32)
    return jnp.where(far <= both, 2 * far - left, far + both)


def arrival(z, slot, cols):
    both = jnp.minimum(z, cols - 1 - z)
    paired = slot <= 2 * both
    far = jnp.where(paired, (slot + 1) // 2, slot - both)
    left = jnp.where(paired, slot % 2, (2 * z >= cols).astype(jnp.int32))
    return z + far - 2 * far * left, left


def kernel(
    planes, cols, point_count,
    feat_hbm, coef_hbm, grads_ref, rec_ref,
    feat_ref, coef_ref, in_s,
    rows, buf, info, norms, mom, tot, part, part_in, whole_grads,
    gram, gram_in, agop, rec_out, rec_in,
    line_s, sib_s, sib_r, info_s, info_r, blk_s, blk_r, diag_s, diag_r,
    part_s, part_r, gram_s, gram_r, agop_s, agop_r, rec_s, rec_r,
):
    load_feats = pltpu.make_async_copy(feat_hbm, feat_ref, in_s.at[0])
    load_coefs = pltpu.make_async_copy(coef_hbm, coef_ref, in_s.at[1])
    load_feats.start()
    load_coefs.start()
    count, width = feat_ref.shape
    gamma = 2.0 / width
    half = width // 2
    chips = planes * cols
    row = lax.axis_index("row")
    z = lax.axis_index("col")
    p, core = lax.div(row, 2), lax.rem(row, 2)
    peers = [(d, k) for k in range(cols) for d in range(planes) if (d, k) != (0, 0)]

    def chip(d, k):
        return (flipped(p, d) * 2 + core, flipped(z, k))

    sibling = (flipped(row, 1), z)

    def copy(src, dst, send, recv, device):
        return pltpu.make_async_remote_copy(
            src_ref=src, dst_ref=dst, send_sem=send, recv_sem=recv,
            device_id=device, device_id_type=MESH,
        )

    barrier = pltpu.get_barrier_semaphore()
    relay = planes == 4
    beside = (1, 2) if relay else range(1, planes)

    def greet(device):
        pl.semaphore_signal(barrier, inc=1, device_id=device, device_id_type=MESH)

    greet(sibling)
    for e in beside:
        greet(chip(e, 0))
    pl.when(z > 0)(lambda: greet((row, z - 1)))
    pl.when(z < cols - 1)(lambda: greet((row, z + 1)))

    load_feats.wait()
    load_coefs.wait()
    own_full = feat_ref[...].astype(jnp.float32)
    own_norms = jnp.sum(own_full * own_full, axis=1, keepdims=True)
    info[0, 0, 0:1, :] = coef_ref[...].astype(jnp.float32)
    info[0, 0, 1:2, :] = jnp.transpose(jnp.broadcast_to(own_norms, (count, 128)))[0:1, :]
    rows[pl.ds(core, 1)] = feat_ref[...][None]
    mom[...] = jnp.zeros_like(mom)
    tot[...] = jnp.zeros_like(tot)
    on_line = (z > 0).astype(jnp.int32) + (z < cols - 1).astype(jnp.int32)
    pl.semaphore_wait(barrier, 1 + len(beside) + on_line)

    sent = []

    def send(*args):
        made = copy(*args)
        made.start()
        sent.append(made)
        return made

    from_sib = send(feat_ref, rows.at[core], sib_s, sib_r, sibling)
    blocks, diagonals, infos = {}, {}, {}

    def spread(k):
        for e in beside:
            infos[e, k] = send(
                info.at[0, k], info.at[e, k], info_s.at[e, k], info_r.at[e, k], chip(e, 0)
            )
            source = feat_ref if k == 0 else buf.at[0, k]
            blocks[e, k] = send(source, buf.at[e, k], blk_s.at[e, k], blk_r.at[e, k], chip(e, 0))

    def forward(k):
        upper, lower = pl.ds(0, count // 2), pl.ds(count // 2, count // 2)
        infos[1, k].wait_recv()
        infos[3, k] = send(
            info.at[1, k], info.at[3, k], info_s.at[3, k], info_r.at[3, k], chip(2, 0)
        )
        blocks[1, k].wait_recv()
        blocks[3, k] = send(
            buf.at[1, k, upper], buf.at[3, k, upper], blk_s.at[3, k], blk_r.at[3, k], chip(2, 0)
        )
        blocks[2, k].wait_recv()
        diagonals[k] = send(
            buf.at[2, k, lower], buf.at[3, k, lower], diag_s.at[k], diag_r.at[k], chip(1, 0)
        )

    def along(k, block, to, sem):
        slot = slot_of(to, block, cols)
        facts = copy(info.at[0, k], info.at[0, slot], sem(1), info_r.at[0, slot], (row, to))
        source = feat_ref if k == 0 else buf.at[0, k]
        return facts, copy(source, buf.at[0, slot], sem(0), blk_r.at[0, slot], (row, to))

    def line(do):
        def to_right():
            for made in along(0, z, z + 1, lambda at: line_s.at[0, at]):
                do(made)

        def to_left():
            for made in along(0, z, z - 1, lambda at: line_s.at[1, at]):
                do(made)

        pl.when(z < cols - 1)(to_right)
        pl.when(z > 0)(to_left)

    def onward(k, do):
        block, left = arrival(z, k, cols)
        to = z - 1 + 2 * left

        def both():
            for made in along(k, block, to, lambda at: (info_s if at else blk_s).at[0, k]):
                do(made)

        pl.when(jnp.logical_and(to >= 0, to < cols))(both)

    def arrived(k):
        copy(info.at[0, 0], info.at[0, k], info_s.at[0, k], info_r.at[0, k], sibling).wait_recv()
        copy(feat_ref, buf.at[0, k], blk_s.at[0, k], blk_r.at[0, k], sibling).wait_recv()

    line(lambda made: made.start())
    spread(0)

    from_sib.wait_recv()
    both = rows[...].reshape(2 * count, width)
    both_full = both.astype(jnp.float32)
    norms[...] = jnp.sum(both_full * both_full, axis=1, keepdims=True)

    def add_block(points, facts):
        coefs = facts[0:1, :]
        col_norms = facts[1:2, :]
        products = lax.dot_general(
            rows[...].reshape(2 * count, width), points, NT, preferred_element_type=jnp.float32
        )
        kern = jnp.exp(-(norms[...] + col_norms - 2.0 * products) * gamma).astype(jnp.bfloat16)
        tall = jnp.transpose(jnp.broadcast_to(coefs, (128, count)))[:, 0:1]
        weighted = (tall * points.astype(jnp.float32)).astype(jnp.bfloat16)
        tot[...] += kern.astype(jnp.float32) * coefs
        mom[...] += jnp.dot(kern, weighted, preferred_element_type=jnp.float32)

    add_block(feat_ref[...], info[0, 0])
    if relay:
        def take(d, k):
            if d > 1:
                infos[d, k].wait_recv()
            if d == 3:
                blocks[d, k].wait_recv()
                diagonals[k].wait_recv()
            add_block(buf[d, k], info[d, k])

        for k in range(1, cols + 1):
            if k < cols:
                arrived(k)
                onward(k, lambda made: made.start())
                spread(k)
            forward(k - 1)
            if k < cols:
                take(0, k)
            take(1, k - 1)
            take(2, k - 1)
            if k > 1:
                take(3, k - 2)
        take(3, cols - 1)
    else:
        for k in range(1, cols):
            arrived(k)
            onward(k, lambda made: made.start())
            spread(k)
        for d, k in peers:
            if d:
                infos[d, k].wait_recv()
                blocks[d, k].wait_recv()

        @pl.loop(1, chips)
        def _(at):
            d, k = lax.div(at, cols), lax.rem(at, cols)
            add_block(buf[d, k], info[d, k])

    totals = jnp.sum(tot[...], axis=1, keepdims=True)
    part[...] = mom[...] - totals * rows[...].reshape(2 * count, width).astype(jnp.float32)
    send(part, part_in, part_s, part_r, sibling).wait_recv()
    both_grads = (2.0 * gamma * (part[...] + part_in[...])).astype(jnp.bfloat16)
    whole_grads[...] = both_grads
    grads_ref[...] = whole_grads[pl.ds(pl.multiple_of(core * count, count), count), :]

    owners, depth = gram.shape[0], gram.shape[1]
    mine = pl.ds(pl.multiple_of(core * half, half), half)
    product = lax.dot_general(
        whole_grads[:, mine], whole_grads[...], TN, preferred_element_type=jnp.float32
    )
    gram[...] = product.reshape(owners, depth, width)

    me = p * cols + z
    every = owners == chips

    def owning(index, do):
        if every:
            do()
        else:
            pl.when(index < owners)(do)

    def place(index):
        return index if every else lax.rem(index, owners)

    def gram_copy(d, k):
        return copy(
            gram.at[place(flipped(p, d) * cols + flipped(z, k))], gram_in.at[d, k],
            gram_s.at[d, k], gram_r.at[d, k], chip(d, k),
        )

    def agop_copy(d, k):
        at = agop.at[place(me)]
        return copy(at, at, agop_s.at[d, k], agop_r.at[d, k], chip(d, k))

    def strip(d):
        return pl.ds(flipped(p, d) * cols, cols)

    if every:
        planar = [
            send(gram.at[strip(e)], gram_in.at[e], gram_s.at[e, 0], gram_r.at[e, 0], chip(e, 0))
            for e in range(1, planes)
        ]
        for e, made in enumerate(planar, 1):
            made.wait_recv()
            gram[strip(0)] += gram_in[e]
        lined = [
            send(gram.at[p * cols + flipped(z, k)], gram_in.at[0, k],
                 gram_s.at[0, k], gram_r.at[0, k], chip(0, k))
            for k in range(1, cols)
        ]
        total = gram[me]
        for k, made in enumerate(lined, 1):
            made.wait_recv()
            total += gram_in[0, k]
        agop[me] = (total / point_count).astype(jnp.bfloat16)
        back = [agop_copy(0, k) for k in range(1, cols)]
        for made in back:
            made.start()
        for made in back:
            made.wait_recv()
        for e in range(1, planes):
            back.append(copy(
                agop.at[strip(0)], agop.at[strip(0)],
                agop_s.at[e, 0], agop_r.at[e, 0], chip(e, 0),
            ))
            back[-1].start()
        for made in back[cols - 1:]:
            made.wait_recv()
        sent.extend(back)
    else:
        for d, k in peers:
            owning(flipped(p, d) * cols + flipped(z, k), gram_copy(d, k).start)

        def reduce_own():
            total = gram[place(me)]
            for d, k in peers:
                gram_copy(d, k).wait_recv()
                total += gram_in[d, k]
            agop[place(me)] = (total / point_count).astype(jnp.bfloat16)
            for d, k in peers:
                agop_copy(d, k).start()

        owning(me, reduce_own)
        for d, k in peers:
            owning(flipped(p, d) * cols + flipped(z, k), agop_copy(d, k).wait_recv)

    colored = lax.dot_general(
        rows[...].reshape(2 * count, width), agop[...].reshape(half, width), NT,
        preferred_element_type=jnp.float32,
    ).astype(jnp.bfloat16).reshape(2, count, half)
    rec_out[...] = colored
    swap = send(rec_out.at[1 - core], rec_in, rec_s, rec_r, sibling)
    rec_ref[:, mine] = rec_out[core]
    swap.wait_recv()
    rec_ref[:, pl.ds(pl.multiple_of((1 - core) * half, half), half)] = rec_in[...]

    for made in sent:
        made.wait_send()
    line(lambda made: made.wait_send())
    for k in range(1, cols):
        onward(k, lambda made: made.wait_send())
    if not every:
        for d, k in peers:
            owning(flipped(p, d) * cols + flipped(z, k), gram_copy(d, k).wait_send)

        def agop_sent():
            for d, k in peers:
                agop_copy(d, k).wait_send()

        owning(me, agop_sent)


def local(planes, cols, features, coefs):
    count, width = features.shape
    chips = planes * cols
    half = width // 2
    owners = min(chips, half // 16)
    depth = half // owners
    bf16, f32 = jnp.bfloat16, jnp.float32
    dma = pltpu.SemaphoreType.DMA
    vmem = pltpu.VMEM
    return pl.pallas_call(
        functools.partial(kernel, planes, cols, count * chips * 2),
        out_shape=[jax.ShapeDtypeStruct((count, width), bf16)] * 2,
        in_specs=[pl.BlockSpec(memory_space=pl.ANY)] * 2,
        out_specs=[pl.BlockSpec(memory_space=vmem)] * 2,
        scratch_shapes=[
            vmem((count, width), bf16),
            vmem((1, count), bf16),
            dma((2,)),
            vmem((2, count, width), bf16),
            vmem((planes, cols, count, width), bf16),
            vmem((planes, cols, 2, count), f32),
            vmem((2 * count, 1), f32),
            vmem((2 * count, width), f32),
            vmem((2 * count, count), f32),
            vmem((2 * count, width), f32),
            vmem((2 * count, width), f32),
            vmem((2 * count, width), bf16),
            vmem((owners, depth, width), f32),
            vmem((planes, cols, depth, width), f32),
            vmem((owners, depth, width), bf16),
            vmem((2, count, half), bf16),
            vmem((count, half), bf16),
            dma((2, 2)),
            dma(()), dma(()),
            dma((planes, cols)), dma((planes, cols)),
            dma((planes, cols)), dma((planes, cols)),
            dma((cols,)), dma((cols,)),
            dma(()), dma(()),
            dma((planes, cols)), dma((planes, cols)),
            dma((planes, cols)), dma((planes, cols)),
            dma(()), dma(()),
        ],
        compiler_params=pltpu.CompilerParams(
            collective_id=0, has_side_effects=True, vmem_limit_bytes=40 * 1024 * 1024
        ),
        cost_estimate=pl.CostEstimate(
            flops=8 * count * count * chips * width,
            bytes_accessed=6 * count * width,
            transcendentals=2 * count * count * chips,
        ),
    )(features, coefs.reshape(1, count))


def solution(mesh):
    return jax.shard_map(
        functools.partial(local, mesh.shape["row"] // 2, mesh.shape["col"]),
        mesh=mesh,
        in_specs=(P(("row", "col"), None), P(("row", "col"))),
        out_specs=(P(("row", "col"), None), P(("row", "col"), None)),
        check_vma=False,
    )
```
